512 devices in a mesh: rep: 16 (over z_hi, x, core), exp: 32 (over y, z_lo).
Axes of the slice: x: 4, y: 4, z: 16 (z_hi: 2, z_lo: 8; z = z_hi * 8 + z_lo), core: 2. Of those that a mesh axis runs over, the one named last changes fastest.
Arguments:
- tokens: bfloat16 [65536, 2048], P(('rep', 'exp')), may hold values from -6 to 6
- routes: int32 [65536, 2], P(('rep', 'exp')), may hold values from 0 to 31, all different within a row; in each aligned block of 128 rows (0 to 127, 128 to 255, ...) at most 12 rows name the same one
- route_weight: float32 [65536, 2], P(('rep', 'exp')), may hold values from 0.2 to 1
- gate_up_store: bfloat16 [32, 2048, 1536], P('exp', 'rep'), may hold values from -0.125 to 0.125
- down_store: bfloat16 [32, 768, 2048], P('exp', None, 'rep'), may hold values from -0.21875 to 0.21875
- held_bucket: int32 [16], replicated, may hold values from 0 to 15, each once
Outputs:
- mixed: bfloat16 [65536, 2048], P(('rep', 'exp'))
The draws below stay inside these ranges and needn't reach their ends.
Inputs may be any that keep to these rules, and one draw needn't show every extreme that they name: `routes`: each token names 2 different experts; within the tokens of one device (aligned blocks of 128 tokens) no expert is named more than 12 times, a bound that some block reaches. `held_bucket`: every bucket is owned by exactly one replica index.
All inputs are finite; a program needn't handle non-finite values.
Results may differ from the reference program's by a relative error of at most 0.0057.
Values may be sent and summed in bfloat16 or wider, within the bound.
A program may use at most 64 MiB of HBM per device.

```python
import math
import jax
import jax.numpy as jnp
import numpy as np
from jax import lax

D = 2048
H = 768
TOP_WIN = 2
TOK_DEV = 128
EXPERTS = 32
CAP = 12
DB = 128
TOKENS = 65536
N_REP = 16
N_EXP = 32


def level_of(key, extent, split, smallest, largest):
    def one(position, shards_of):
        draws = jax.random.uniform(jax.random.fold_in(jax.random.fold_in(key, 6), position), (shards_of,), jnp.float32, smallest / len(split), largest / len(split))
        return jnp.repeat(jnp.exp(draws), extent[position] // shards_of).reshape((-1,) + (1,) * (len(extent) - position - 1))

    gain = one(*split[0])
    for cut in split[1:]:
        gain = gain * one(*cut)
    return gain


def deal_out(own_key, own, number, rows, number_of, top, reach, lean):
    ranking = jax.random.permutation(own_key, number_of)
    crowded, common = load_shares(number_of, rows * top, reach, lean, True), load_shares(number_of, rows * top, reach, lean, False)
    places = jnp.arange(number_of)

    def named(lengths, offset_by):
        used = int((lengths > 0).sum())
        fixed = max(1, used // 4)
        shifted = fixed + (places - fixed + offset_by * (used - fixed)) % max(1, number_of - fixed)
        return jnp.zeros((number_of,), jnp.int32).at[ranking[jnp.where(places < fixed, places, shifted)]].set(jnp.asarray(lengths, jnp.int32))

    lengths = jnp.where(number % 4 == 0, named(crowded, number // 4), named(common, number - number // 4 - 1))
    mixed = jax.random.permutation(jax.random.fold_in(own, 3), number_of)
    giver, receiver = mixed[0:number_of // 2 * 2:2], mixed[1:number_of // 2 * 2:2]
    margin = jnp.minimum(lengths[giver] - 1, reach - lengths[receiver]) // 2
    margin = jnp.where((giver == ranking[0]) | (receiver == ranking[0]) | (lengths[receiver] == 0), 0, jnp.maximum(margin, 0))
    shifted = jax.random.randint(jax.random.fold_in(own, 4), (number_of // 2,), 0, 1 << 20) % (margin + 1)
    lengths = lengths.at[giver].add(-shifted).at[receiver].add(shifted)
    items = jnp.searchsorted(jnp.cumsum(lengths), jnp.arange(rows * top), side="right").astype(jnp.int32)
    listing = items.reshape(top, rows).T
    listing = listing[jax.random.permutation(jax.random.fold_in(own, 1), rows)]
    offset_by = jax.random.randint(jax.random.fold_in(own, 2), (rows, 1), 0, top)
    return jnp.take_along_axis(listing, (jnp.arange(top)[None, :] + offset_by) % top, axis=1)


def load_shares(amount, total, reach, lean, full):
    weights = [(1 << 20) // math.isqrt(rank ** lean) + 1 for rank in range(1, amount + 1)]
    largest = reach if full else min(reach, max(-(-total // amount), total * weights[0] // sum(weights)))
    least = 1 if total - largest >= amount - 1 else 0
    holding, rest = [largest] + [least] * (amount - 1), total - largest - least * (amount - 1)
    while rest > 0:
        movable = [i for i in range(1, amount) if holding[i] < largest] or [i for i in range(1, amount) if holding[i] < reach]
        pool, budget = sum([weights[i] for i in movable]), rest
        for i in movable:
            addition = min(reach - holding[i], max(1, budget * weights[i] // pool), rest)
            holding[i] = holding[i] + addition
            rest = rest - addition
    return np.array(holding)


def normal_values(own_key, dims, spread, bound, shards=(), kind=jnp.bfloat16):
    result = spread * jax.random.normal(own_key, dims, jnp.float32)
    if shards:
        result = result * level_of(own_key, dims, shards, -0.22, 0.18)
    return jnp.clip(result, -bound, bound).astype(kind)


def setup_inputs(seed: int = 0) -> dict:
    key_of = jax.random.split(jax.random.key(seed), 7)
    tokens = normal_values(key_of[0], (TOKENS, D), 1.0, 6.0, ((0, 512),))
    routes_keys = jax.random.split(jax.random.fold_in(key_of[1], 1), TOKENS // TOK_DEV)
    routes_turns = jax.random.permutation(jax.random.fold_in(key_of[1], 3), TOKENS // TOK_DEV)
    routes = jax.vmap(lambda own, number: deal_out(jax.random.fold_in(key_of[1], 2), own, number, TOK_DEV, EXPERTS, TOP_WIN, CAP, 2))(routes_keys, routes_turns).reshape((TOKENS, TOP_WIN))
    route_weight = jnp.clip(0.2 + 0.8 * jax.random.uniform(key_of[2], (TOKENS, TOP_WIN), jnp.float32) ** level_of(key_of[2], (TOKENS, TOP_WIN), ((0, 512),), -0.2, 0.2), 0.2, 1.0)
    gate_up_store = normal_values(key_of[3], (EXPERTS, D, 2 * H), D ** -0.5, 0.125, ((0, 32), (1, 16)))
    down_store = normal_values(key_of[4], (EXPERTS, H, D), H ** -0.5, 0.21875, ((0, 32), (2, 16)))
    held_bucket = jax.random.permutation(key_of[5], N_REP).astype(jnp.int32)
    return {"tokens": tokens, "routes": routes, "route_weight": route_weight, "gate_up_store": gate_up_store, "down_store": down_store, "held_bucket": held_bucket}


def reference(tokens, routes, route_weight, gate_up_store, down_store, held_bucket):
    bucket_count = held_bucket.shape[0]
    inverse = jnp.zeros((bucket_count,), jnp.int32).at[held_bucket].set(jnp.arange(bucket_count, dtype=jnp.int32))
    gate_up = jnp.take(gate_up_store.reshape(EXPERTS, bucket_count, DB, 2 * H), inverse, axis=1).reshape(EXPERTS, D, 2 * H)
    down_proj = jnp.take(down_store.reshape(EXPERTS, H, bucket_count, DB), inverse, axis=2).reshape(EXPERTS, H, D)
    flat_routes = routes.reshape(-1)
    route_total = flat_routes.shape[0]
    onehot = (flat_routes[:, None] == jnp.arange(EXPERTS, dtype=jnp.int32)[None, :]).astype(jnp.int32)
    slot_rank = jnp.sum((jnp.cumsum(onehot, axis=0, dtype=jnp.int32) - onehot) * onehot, axis=1, dtype=jnp.int32)
    slot_depth = N_REP * N_EXP * CAP
    route_table = jnp.full((EXPERTS, slot_depth), route_total, jnp.int32).at[flat_routes, slot_rank].set(jnp.arange(route_total, dtype=jnp.int32))
    padded_tokens = jnp.concatenate([tokens, jnp.zeros((1, D), tokens.dtype)], axis=0)
    padded_weight = jnp.concatenate([route_weight.reshape(-1), jnp.zeros((1,), route_weight.dtype)])

    def one_expert(running, expert):
        chosen = route_table[expert]
        token_index = (chosen // TOP_WIN).astype(jnp.int32)
        row_block = padded_tokens[token_index]
        pre_act = jnp.dot(row_block, gate_up[expert], preferred_element_type=jnp.float32)
        hidden = (jax.nn.silu(pre_act[:, :H]) * pre_act[:, H:]).astype(jnp.bfloat16)
        produced = jnp.dot(hidden, down_proj[expert], preferred_element_type=jnp.float32).astype(jnp.bfloat16)
        update = padded_weight[chosen][:, None] * produced.astype(jnp.float32)
        return running.at[token_index].add(update, mode="drop"), None

    zero_sum = jnp.zeros((TOKENS, D), jnp.float32)
    summed, unused_out = lax.scan(one_expert, zero_sum, jnp.arange(EXPERTS, dtype=jnp.int32))
    return summed.astype(jnp.bfloat16)
```

```python
import functools

import jax
import jax.numpy as jnp
from jax import lax
from jax.experimental import pallas as pl
from jax.experimental.pallas import tpu as pltpu
from jax.sharding import PartitionSpec as P

MESH = pl.DeviceIdType.MESH
D = 2048
H = 768
TOK = 128
DB = 128
NR = 16
PK = 16
PW = 1536
SLOTS = 32
ROWS = SLOTS * PK
STEPS = (4, 3, -3, 2, -2, 1, -1, 0)
GROUPS = ((0, 12), (12, 20), (20, 32))
SELF = 28
CH = 3
BF = jnp.bfloat16
F32 = jnp.float32


def dot(a, b):
    return jnp.dot(a, b, preferred_element_type=F32)


def kernel(
    held, tok, routes, weight, gu, dn, out,
    gu_all, dn_all, tperm, opk, rcv, ppk, ret, wmix, xbuf, hid, p3, phi,
    loc, zs, zr, xs, xr, cs, cr, ds, dr, rs, rr,
):
    rep = lax.axis_index("rep")
    ex = lax.axis_index("exp")
    c = rep % 2
    x = (rep // 2) % 4
    zh = rep // 8
    y = ex // 8
    z = zh * 8 + ex % 8

    def dev(ax, ay, az, ac):
        ax = (ax + 4) % 4
        ay = (ay + 4) % 4
        az = (az + 16) % 16
        return (((az // 8) * 4 + ax) * 2 + ac, ay * 8 + az % 8)

    def owner(azh, ax, ac):
        return (azh * 4 + (ax + 4) % 4) * 2 + ac

    def disp(k):
        return 4 - 8 * c if STEPS[k] == 4 else STEPS[k]

    partners = [dev(x, y, z + 8, c), dev(x, y, z, 1 - c)]
    partners += [dev(x + k, y, z, c) for k in (1, 2, 3)]
    for d in range(-4, 5):
        for dy in range(4):
            if d or dy:
                partners.append(dev(x, y + dy, z + d, c))
    barrier = pltpu.get_barrier_semaphore()
    for p in partners:
        pl.semaphore_signal(barrier, inc=1, device_id=p, device_id_type=MESH)
    pl.semaphore_wait(barrier, len(partners))

    mine = owner(zh, x, c)
    far = owner(1 - zh, x, c)

    def own(ch):
        return dn if ch == 2 else gu.at[pl.ds(64 * ch, 64)]

    def slot(r, ch):
        if ch == 2:
            return dn_all.at[r]
        return gu_all.at[pl.ds(pl.multiple_of(r * DB + 64 * ch, 64), 64)]

    def send(src, dst, ss, rsem, to):
        return pltpu.make_async_remote_copy(
            src_ref=src, dst_ref=dst, send_sem=ss, recv_sem=rsem,
            device_id=to, device_id_type=MESH,
        )

    started = []

    def go(cp):
        cp.start()
        started.append(cp)

    def arrived(dst, ss, rsem, to):
        send(dst, dst, ss, rsem, to).wait_recv()

    core = dev(x, y, z, 1 - c)
    for ch in range(CH):
        go(send(own(ch), slot(mine, ch), zs.at[ch], zr.at[ch], dev(x, y, z + 8, c)))
    for ch in range(CH):
        for k in (1, 3, 2):
            i = ch * 3 + k - 1
            go(send(own(ch), slot(mine, ch), xs.at[i], xr.at[i], dev(x + k, y, z, c)))
    for ch in range(CH):
        go(send(own(ch), slot(mine, ch), cs.at[ch], cr.at[ch], core))
    keep = [pltpu.make_async_copy(own(ch), slot(mine, ch), loc.at[ch]) for ch in range(CH)]
    for cp in keep:
        cp.start()

    for r in range(NR):
        pick = tok[:, 0:DB]
        for b in range(1, NR):
            pick = jnp.where(held[r] == b, tok[:, b * DB : (b + 1) * DB], pick)
        tperm[:, r * DB : (r + 1) * DB] = pick

    lane = lax.broadcasted_iota(jnp.int32, (TOK, 128), 1)
    row = lax.broadcasted_iota(jnp.int32, (TOK, 128), 0)
    lower = (lane < row).astype(F32).astype(BF)

    def column(v):
        return jnp.transpose(jnp.broadcast_to(v, (128, TOK)))

    named = [column(routes[k : k + 1, :].astype(F32)) for k in range(2)]
    share = [column(weight[k : k + 1, :]) for k in range(2)]
    hot0 = (lane.astype(F32) == named[0]).astype(F32)
    hot1 = (lane.astype(F32) == named[1]).astype(F32)
    seen0 = dot(lower, hot0.astype(BF))
    seen1 = dot(lower, hot1.astype(BF)) + jnp.sum(hot0, axis=0, keepdims=True)
    lanef = lane.astype(F32)
    wide = lax.broadcasted_iota(jnp.int32, (TOK, ROWS), 1).astype(F32)
    tall = row.astype(F32)
    keys = []
    for hot, seen in ((hot0, seen0), (hot1, seen1)):
        base = jnp.sum(hot * lanef, axis=1, keepdims=True) * PK
        rank = jnp.sum(hot * seen, axis=1, keepdims=True)
        quad = (rank >= 4.0).astype(F32) + (rank >= 8.0).astype(F32)
        keys.append((base + rank, base + 12.0 + rank - 4.0 * quad, quad))
    for j in range(4):
        mix = jnp.zeros((TOK, ROWS), F32)
        for k, (lo, hi, quad) in enumerate(keys):
            key = lo if j == 3 else jnp.where(quad == float(j), hi, -1.0)
            mix = mix + jnp.where(wide == key, share[k][:, 0:1], 0.0)
        top = mix.astype(BF)
        wmix[j, 0:TOK, :] = top
        wmix[j, TOK : 2 * TOK, :] = (mix - top.astype(F32)).astype(BF)
    turned = []
    for lo, hi, quad in keys:
        turned.append(
            tuple(jnp.transpose(jnp.broadcast_to(v, (TOK, 128))) for v in (lo, hi, quad))
        )
    for b in range(ROWS // 128):
        at = tall + float(b * 128)
        low = jnp.zeros((128, TOK), F32)
        for lo, hi, quad in turned:
            low = low + (at == lo).astype(F32)
        for j in range(3):
            high = jnp.zeros((128, TOK), F32)
            for lo, hi, quad in turned:
                high = high + (at == jnp.where(quad == float(j), hi, -1.0)).astype(F32)
            block = dot(low.astype(BF), tperm[:, 512 * j : 512 * (j + 1)])
            block = block + dot(high.astype(BF), tperm[:, PW:D])
            opk[b * 128 : (b + 1) * 128, 512 * j : 512 * (j + 1)] = block.astype(BF)

    def expert(k, dy):
        return ((y + dy) % 4) * 8 + (z + disp(k) + 16) % 8

    def tile(ref, e):
        return ref.at[pl.ds(pl.multiple_of(e * PK, PK), PK)]

    def dispatch(first, last):
        for i in range(first, last):
            if i == SELF:
                continue
            k, dy = i // 4, i % 4
            go(send(
                tile(opk, expert(k, dy)), tile(rcv, i), ds.at[i], dr.at[i],
                dev(x, y + dy, z + disp(k), c),
            ))

    def from_x(ch, part):
        for k in (1, 3, 2):
            i = part * 9 + ch * 3 + k - 1
            r = owner(zh if part == 0 else 1 - zh, x - k, c)
            arrived(slot(r, ch), xs.at[i], xr.at[i], dev(x + k, y, z, c))
            n = 6 + i
            go(send(slot(r, ch), slot(r, ch), cs.at[n], cr.at[n], core))

    for ch in range(CH):
        from_x(ch, 0)
        arrived(slot(far, ch), zs.at[ch], zr.at[ch], dev(x, y, z + 8, c))
        for k in (1, 3, 2):
            i = 9 + ch * 3 + k - 1
            go(send(slot(far, ch), slot(far, ch), xs.at[i], xr.at[i], dev(x + k, y, z, c)))
        go(send(slot(far, ch), slot(far, ch), cs.at[3 + ch], cr.at[3 + ch], core))
        if ch == 1:
            dispatch(0, SLOTS)
            rcv[SELF * PK : (SELF + 1) * PK, :] = opk[pl.ds(pl.multiple_of(ex * PK, PK), PK), :]
    for ch in range(CH):
        from_x(ch, 1)
    for ch in range(CH):
        arrived(slot(owner(zh, x, 1 - c), ch), cs.at[ch], cr.at[ch], core)
        arrived(slot(owner(1 - zh, x, 1 - c), ch), cs.at[3 + ch], cr.at[3 + ch], core)
        for part in range(2):
            for k in (1, 2, 3):
                n = 6 + part * 9 + ch * 3 + k - 1
                r = owner(zh if part == 0 else 1 - zh, x - k, 1 - c)
                arrived(slot(r, ch), cs.at[n], cr.at[n], core)
    for cp in keep:
        cp.wait()

    for first, last in GROUPS:
        n = (last - first) * PK
        lo = first * PK
        for i in range(first, last):
            if i == SELF:
                continue
            k, dy = i // 4, i % 4
            arrived(tile(rcv, i), ds.at[i], dr.at[i], dev(x, y + dy, z + disp(k), c))
        a = lax.broadcasted_iota(jnp.int32, (n, n), 0)
        b = lax.broadcasted_iota(jnp.int32, (n, n), 1)
        same = (a // PK) == (b // PK)
        ai, bi = a % PK, b % PK
        xbuf[0:n, 0:PW] = rcv[lo : lo + n, :]
        tail = jnp.zeros((n, 512), F32)
        for j in range(3):
            take = same & (ai // 4 == j) & (bi == 12 + ai % 4)
            tail = tail + dot(
                take.astype(F32).astype(BF), rcv[lo : lo + n, 512 * j : 512 * (j + 1)]
            )
        xbuf[0:n, PW:D] = tail.astype(BF)

        def up(t, carry):
            col = pl.multiple_of(t * 256, 256)
            g = dot(xbuf[0:n, :], gu_all[:, pl.ds(col, 256)])
            u = dot(xbuf[0:n, :], gu_all[:, pl.ds(pl.multiple_of(H + col, 256), 256)])
            hid[0:n, pl.ds(col, 256)] = (g / (1.0 + jnp.exp(-g)) * u).astype(BF)
            return carry

        lax.fori_loop(0, 3, up, 0)

        def down(q):
            w = jnp.concatenate([dn_all[2 * q], dn_all[2 * q + 1]], axis=1)
            return dot(hid[0:n, :], w).astype(BF)

        for q in (6, 7):
            p3[0:n, (q - 6) * 256 : (q - 5) * 256] = down(q)
        for j in range(3):
            put = same & (bi // 4 == j) & (ai == 12 + bi % 4)
            phi[0:n, 512 * j : 512 * (j + 1)] = dot(
                put.astype(F32).astype(BF), p3[0:n, :]
            ).astype(BF)
        real = lax.broadcasted_iota(jnp.int32, (n, 256), 0) % PK < 12

        def pack(q, carry):
            col = pl.multiple_of(q * 256, 256)
            v = jnp.where(real, down(q).astype(F32), phi[0:n, pl.ds(col, 256)].astype(F32))
            ppk[lo : lo + n, pl.ds(col, 256)] = v.astype(BF)
            return carry

        lax.fori_loop(0, 6, pack, 0)
        for i in range(first, last):
            if i == SELF:
                continue
            k, dy = i // 4, i % 4
            go(send(
                tile(ppk, i), tile(ret, ex), rs.at[i], rr.at[i],
                dev(x, y - dy, z - disp(k), c),
            ))
    ret[pl.ds(pl.multiple_of(ex * PK, PK), PK), :] = ppk[SELF * PK : (SELF + 1) * PK, :]

    for i in range(SLOTS):
        if i == SELF:
            continue
        k, dy = i // 4, i % 4
        arrived(tile(ret, expert(k, dy)), rs.at[i], rr.at[i], dev(x, y - dy, z - disp(k), c))

    last = jnp.zeros((2 * TOK, 512), F32)
    for j in range(3):
        block = ret[:, 512 * j : 512 * (j + 1)]
        m = dot(wmix[3], block)
        out[:, 512 * j : 512 * (j + 1)] = (m[0:TOK] + m[TOK : 2 * TOK]).astype(BF)
        last = last + dot(wmix[j], block)
    out[:, PW:D] = (last[0:TOK] + last[TOK : 2 * TOK]).astype(BF)

    for cp in started:
        cp.wait_send()


def restore(held, mixed, out):
    for r in range(NR):
        col = pl.multiple_of(held[r] * DB, DB)
        out[:, pl.ds(col, DB)] = mixed[:, r * DB : (r + 1) * DB]


def local(tokens, routes, route_weight, gate_up_store, down_store, held_bucket):
    vmem = pl.BlockSpec(memory_space=pltpu.VMEM)
    dma = pltpu.SemaphoreType.DMA
    most = max(b - a for a, b in GROUPS) * PK
    mixed = pl.pallas_call(
        kernel,
        out_shape=jax.ShapeDtypeStruct((TOK, D), BF),
        in_specs=[pl.BlockSpec(memory_space=pltpu.SMEM)] + [vmem] * 5,
        out_specs=vmem,
        scratch_shapes=[
            pltpu.VMEM((D, 2 * H), BF),
            pltpu.VMEM((NR, H, DB), BF),
            pltpu.VMEM((TOK, D), BF),
            pltpu.VMEM((ROWS, PW), BF),
            pltpu.VMEM((ROWS, PW), BF),
            pltpu.VMEM((ROWS, PW), BF),
            pltpu.VMEM((ROWS, PW), BF),
            pltpu.VMEM((4, 2 * TOK, ROWS), BF),
            pltpu.VMEM((most, D), BF),
            pltpu.VMEM((most, H), BF),
            pltpu.VMEM((most, 512), BF),
            pltpu.VMEM((most, PW), BF),
            dma((CH,)),
            dma((CH,)), dma((CH,)),
            dma((18,)), dma((18,)),
            dma((24,)), dma((24,)),
            dma((SLOTS,)), dma((SLOTS,)),
            dma((SLOTS,)), dma((SLOTS,)),
        ],
        compiler_params=pltpu.CompilerParams(
            collective_id=0, has_side_effects=True, vmem_limit_bytes=56 << 20
        ),
        name="layer",
    )(
        held_bucket, tokens, routes.T, route_weight.T,
        gate_up_store.reshape(DB, 2 * H), down_store.reshape(H, DB),
    )
    return pl.pallas_call(
        restore,
        out_shape=jax.ShapeDtypeStruct((TOK, D), BF),
        in_specs=[pl.BlockSpec(memory_space=pltpu.SMEM), vmem],
        out_specs=vmem,
        name="restore",
    )(held_bucket, mixed)


def solution(mesh):
    in_specs = (
        P(("rep", "exp"), None),
        P(("rep", "exp"), None),
        P(("rep", "exp"), None),
        P("exp", "rep", None),
        P("exp", None, "rep"),
        P(),
    )
    out_specs = P(("rep", "exp"), None)
    return jax.shard_map(local, mesh=mesh, in_specs=in_specs, out_specs=out_specs, check_vma=False)
```

```python
import functools

import jax
import jax.numpy as jnp
from jax import lax
from jax.experimental import pallas as pl
from jax.experimental.pallas import tpu as pltpu
from jax.sharding import PartitionSpec as P

MESH = pl.DeviceIdType.MESH
D = 2048
H = 768
TOK = 128
DB = 128
NR = 16
PK = 16
PW = 1536
SLOTS = 32
ROWS = SLOTS * PK
STEPS = (4, 3, -3, 2, -2, 1, -1, 0)
GROUPS = ((0, 12), (12, 20), (20, 32))
MIX = ((0, 16), (16, 32))
SELF = 28
CH = 3
BF = jnp.bfloat16
F32 = jnp.float32


def dot(a, b):
    return jnp.dot(a, b, preferred_element_type=F32)


def kernel(
    held, tok, routes, weight, gu, dn, out,
    gu_all, dn_all, tperm, opk, rcv, ppk, ret, wmix, xbuf, hid, p3, phi, comb,
    loc, zs, zr, xs, xr, cs, cr, ds, dr, rs, rr,
):
    rep = lax.axis_index("rep")
    ex = lax.axis_index("exp")
    c = rep % 2
    x = (rep // 2) % 4
    zh = rep // 8
    y = ex // 8
    z = zh * 8 + ex % 8

    def dev(ax, ay, az, ac):
        ax = (ax + 4) % 4
        ay = (ay + 4) % 4
        az = (az + 16) % 16
        return (((az // 8) * 4 + ax) * 2 + ac, ay * 8 + az % 8)

    def owner(azh, ax, ac):
        return (azh * 4 + (ax + 4) % 4) * 2 + ac

    def disp(k):
        return 4 - 8 * c if STEPS[k] == 4 else STEPS[k]

    partners = [dev(x, y, z + 8, c), dev(x, y, z, 1 - c)]
    partners += [dev(x + k, y, z, c) for k in (1, 2, 3)]
    for d in range(-4, 5):
        for dy in range(4):
            if d or dy:
                partners.append(dev(x, y + dy, z + d, c))
    barrier = pltpu.get_barrier_semaphore()
    for p in partners:
        pl.semaphore_signal(barrier, inc=1, device_id=p, device_id_type=MESH)
    pl.semaphore_wait(barrier, len(partners))

    mine = owner(zh, x, c)
    far = owner(1 - zh, x, c)

    def own(ch):
        return dn if ch == 2 else gu.at[pl.ds(64 * ch, 64)]

    def slot(r, ch):
        if ch == 2:
            return dn_all.at[r]
        return gu_all.at[pl.ds(pl.multiple_of(r * DB + 64 * ch, 64), 64)]

    def send(src, dst, ss, rsem, to):
        return pltpu.make_async_remote_copy(
            src_ref=src, dst_ref=dst, send_sem=ss, recv_sem=rsem,
            device_id=to, device_id_type=MESH,
        )

    started = []

    def go(cp):
        cp.start()
        started.append(cp)

    def arrived(dst, ss, rsem, to):
        send(dst, dst, ss, rsem, to).wait_recv()

    core = dev(x, y, z, 1 - c)
    for ch in range(CH):
        go(send(own(ch), slot(mine, ch), zs.at[ch], zr.at[ch], dev(x, y, z + 8, c)))
    for ch in range(CH):
        for k in (1, 3, 2):
            i = ch * 3 + k - 1
            go(send(own(ch), slot(mine, ch), xs.at[i], xr.at[i], dev(x + k, y, z, c)))
    for ch in range(CH):
        go(send(own(ch), slot(mine, ch), cs.at[ch], cr.at[ch], core))
    keep = [pltpu.make_async_copy(own(ch), slot(mine, ch), loc.at[ch]) for ch in range(CH)]
    for cp in keep:
        cp.start()

    for r in range(NR):
        pick = tok[:, 0:DB]
        for b in range(1, NR):
            pick = jnp.where(held[r] == b, tok[:, b * DB : (b + 1) * DB], pick)
        tperm[:, r * DB : (r + 1) * DB] = pick

    lane = lax.broadcasted_iota(jnp.int32, (TOK, 128), 1)
    row = lax.broadcasted_iota(jnp.int32, (TOK, 128), 0)
    lower = (lane < row).astype(F32).astype(BF)

    def column(v):
        return jnp.transpose(jnp.broadcast_to(v, (128, TOK)))

    named = [column(routes[k : k + 1, :].astype(F32)) for k in range(2)]
    share = [column(weight[k : k + 1, :]) for k in range(2)]
    hot0 = (lane.astype(F32) == named[0]).astype(F32)
    hot1 = (lane.astype(F32) == named[1]).astype(F32)
    seen0 = dot(lower, hot0.astype(BF))
    seen1 = dot(lower, hot1.astype(BF)) + jnp.sum(hot0, axis=0, keepdims=True)
    dz = (lane % 8 - ex % 8 + 8) % 8
    step = jnp.where(dz < 4, 7 - 2 * dz, 2 * dz - 8)
    place = (step * 4 + (lane // 8 - y + 16) % 4).astype(F32)
    wide = lax.broadcasted_iota(jnp.int32, (TOK, ROWS), 1).astype(F32)
    tall = row.astype(F32)
    keys = []
    for hot, seen in ((hot0, seen0), (hot1, seen1)):
        base = jnp.sum(hot * place, axis=1, keepdims=True) * PK
        rank = jnp.sum(hot * seen, axis=1, keepdims=True)
        quad = (rank >= 4.0).astype(F32) + (rank >= 8.0).astype(F32)
        keys.append((base + rank, base + 12.0 + rank - 4.0 * quad, quad))
    for j in range(4):
        mix = jnp.zeros((TOK, ROWS), F32)
        for k, (lo, hi, quad) in enumerate(keys):
            key = lo if j == 3 else jnp.where(quad == float(j), hi, -1.0)
            mix = mix + jnp.where(wide == key, share[k][:, 0:1], 0.0)
        top = mix.astype(BF)
        wmix[j, 0:TOK, :] = top
        wmix[j, TOK : 2 * TOK, :] = (mix - top.astype(F32)).astype(BF)
    turned = []
    for lo, hi, quad in keys:
        turned.append(
            tuple(jnp.transpose(jnp.broadcast_to(v, (TOK, 128))) for v in (lo, hi, quad))
        )
    for b in range(ROWS // 128):
        at = tall + float(b * 128)
        low = jnp.zeros((128, TOK), F32)
        for lo, hi, quad in turned:
            low = low + (at == lo).astype(F32)
        for j in range(3):
            high = jnp.zeros((128, TOK), F32)
            for lo, hi, quad in turned:
                high = high + (at == jnp.where(quad == float(j), hi, -1.0)).astype(F32)
            block = dot(low.astype(BF), tperm[:, 512 * j : 512 * (j + 1)])
            block = block + dot(high.astype(BF), tperm[:, PW:D])
            opk[b * 128 : (b + 1) * 128, 512 * j : 512 * (j + 1)] = block.astype(BF)

    def tile(ref, i):
        return ref.at[pl.ds(i * PK, PK)]

    def dispatch(first, last):
        for i in range(first, last):
            if i == SELF:
                continue
            k, dy = i // 4, i % 4
            go(send(
                tile(opk, i), tile(rcv, i), ds.at[i], dr.at[i],
                dev(x, y + dy, z + disp(k), c),
            ))

    def from_x(ch, part):
        for k in (1, 3, 2):
            i = part * 9 + ch * 3 + k - 1
            r = owner(zh if part == 0 else 1 - zh, x - k, c)
            arrived(slot(r, ch), xs.at[i], xr.at[i], dev(x + k, y, z, c))
            n = 6 + i
            go(send(slot(r, ch), slot(r, ch), cs.at[n], cr.at[n], core))

    for ch in range(CH):
        from_x(ch, 0)
        arrived(slot(far, ch), zs.at[ch], zr.at[ch], dev(x, y, z + 8, c))
        for k in (1, 3, 2):
            i = 9 + ch * 3 + k - 1
            go(send(slot(far, ch), slot(far, ch), xs.at[i], xr.at[i], dev(x + k, y, z, c)))
        go(send(slot(far, ch), slot(far, ch), cs.at[3 + ch], cr.at[3 + ch], core))
        if ch == 1:
            dispatch(0, SLOTS)
            rcv[SELF * PK : (SELF + 1) * PK, :] = opk[SELF * PK : (SELF + 1) * PK, :]
    for ch in range(CH):
        from_x(ch, 1)
    for ch in range(CH):
        arrived(slot(owner(zh, x, 1 - c), ch), cs.at[ch], cr.at[ch], core)
        arrived(slot(owner(1 - zh, x, 1 - c), ch), cs.at[3 + ch], cr.at[3 + ch], core)
        for part in range(2):
            for k in (1, 2, 3):
                n = 6 + part * 9 + ch * 3 + k - 1
                r = owner(zh if part == 0 else 1 - zh, x - k, 1 - c)
                arrived(slot(r, ch), cs.at[n], cr.at[n], core)
    for cp in keep:
        cp.wait()

    for first, last in GROUPS:
        n = (last - first) * PK
        lo = first * PK
        for i in range(first, last):
            if i == SELF:
                continue
            k, dy = i // 4, i % 4
            arrived(tile(rcv, i), ds.at[i], dr.at[i], dev(x, y + dy, z + disp(k), c))
        a = lax.broadcasted_iota(jnp.int32, (n, n), 0)
        b = lax.broadcasted_iota(jnp.int32, (n, n), 1)
        same = (a // PK) == (b // PK)
        ai, bi = a % PK, b % PK
        xbuf[0:n, 0:PW] = rcv[lo : lo + n, :]
        tail = jnp.zeros((n, 512), F32)
        for j in range(3):
            take = same & (ai // 4 == j) & (bi == 12 + ai % 4)
            tail = tail + dot(
                take.astype(F32).astype(BF), rcv[lo : lo + n, 512 * j : 512 * (j + 1)]
            )
        xbuf[0:n, PW:D] = tail.astype(BF)

        def up(t, carry):
            col = pl.multiple_of(t * 256, 256)
            g = dot(xbuf[0:n, :], gu_all[:, pl.ds(col, 256)])
            u = dot(xbuf[0:n, :], gu_all[:, pl.ds(pl.multiple_of(H + col, 256), 256)])
            hid[0:n, pl.ds(col, 256)] = (g / (1.0 + jnp.exp(-g)) * u).astype(BF)
            return carry

        lax.fori_loop(0, 3, up, 0)

        def down(q):
            w = jnp.concatenate([dn_all[2 * q], dn_all[2 * q + 1]], axis=1)
            return dot(hid[0:n, :], w).astype(BF)

        for q in (6, 7):
            p3[0:n, (q - 6) * 256 : (q - 5) * 256] = down(q)
        for j in range(3):
            put = same & (bi // 4 == j) & (ai == 12 + bi % 4)
            phi[0:n, 512 * j : 512 * (j + 1)] = dot(
                put.astype(F32).astype(BF), p3[0:n, :]
            ).astype(BF)
        real = lax.broadcasted_iota(jnp.int32, (n, 256), 0) % PK < 12

        def pack(q, carry):
            col = pl.multiple_of(q * 256, 256)
            v = jnp.where(real, down(q).astype(F32), phi[0:n, pl.ds(col, 256)].astype(F32))
            ppk[lo : lo + n, pl.ds(col, 256)] = v.astype(BF)
            return carry

        lax.fori_loop(0, 6, pack, 0)
        for i in range(first, last):
            if i == SELF:
                continue
            k, dy = i // 4, i % 4
            go(send(
                tile(ppk, i), tile(ret, i), rs.at[i], rr.at[i],
                dev(x, y - dy, z - disp(k), c),
            ))
    ret[SELF * PK : (SELF + 1) * PK, :] = ppk[SELF * PK : (SELF + 1) * PK, :]

    def put(first, cols, m):
        v = m[0:TOK] + m[TOK : 2 * TOK]
        if first == 0:
            comb[:, cols] = v
        else:
            out[:, cols] = (comb[:, cols] + v).astype(BF)

    for first, last in MIX:
        for i in range(first, last):
            if i == SELF:
                continue
            k, dy = i // 4, i % 4
            arrived(tile(ret, i), rs.at[i], rr.at[i], dev(x, y - dy, z - disp(k), c))
        lo, hi = first * PK, last * PK
        part = jnp.zeros((2 * TOK, 512), F32)
        for j in range(3):
            block = ret[lo:hi, 512 * j : 512 * (j + 1)]
            m = dot(wmix[3, :, lo:hi], block)
            part = part + dot(wmix[j, :, lo:hi], block)
            put(first, slice(512 * j, 512 * (j + 1)), m)
        put(first, slice(PW, D), part)

    for cp in started:
        cp.wait_send()


def restore(held, mixed, out):
    for r in range(NR):
        col = pl.multiple_of(held[r] * DB, DB)
        out[:, pl.ds(col, DB)] = mixed[:, r * DB : (r + 1) * DB]


def local(tokens, routes, route_weight, gate_up_store, down_store, held_bucket):
    vmem = pl.BlockSpec(memory_space=pltpu.VMEM)
    dma = pltpu.SemaphoreType.DMA
    most = max(b - a for a, b in GROUPS) * PK
    mixed = pl.pallas_call(
        kernel,
        out_shape=jax.ShapeDtypeStruct((TOK, D), BF),
        in_specs=[pl.BlockSpec(memory_space=pltpu.SMEM)] + [vmem] * 5,
        out_specs=vmem,
        scratch_shapes=[
            pltpu.VMEM((D, 2 * H), BF),
            pltpu.VMEM((NR, H, DB), BF),
            pltpu.VMEM((TOK, D), BF),
            pltpu.VMEM((ROWS, PW), BF),
            pltpu.VMEM((ROWS, PW), BF),
            pltpu.VMEM((ROWS, PW), BF),
            pltpu.VMEM((ROWS, PW), BF),
            pltpu.VMEM((4, 2 * TOK, ROWS), BF),
            pltpu.VMEM((most, D), BF),
            pltpu.VMEM((most, H), BF),
            pltpu.VMEM((most, 512), BF),
            pltpu.VMEM((most, PW), BF),
            pltpu.VMEM((TOK, D), F32),
            dma((CH,)),
            dma((CH,)), dma((CH,)),
            dma((18,)), dma((18,)),
            dma((24,)), dma((24,)),
            dma((SLOTS,)), dma((SLOTS,)),
            dma((SLOTS,)), dma((SLOTS,)),
        ],
        compiler_params=pltpu.CompilerParams(
            collective_id=0, has_side_effects=True, vmem_limit_bytes=28 << 20
        ),
        name="layer",
    )(
        held_bucket, tokens, routes.T, route_weight.T,
        gate_up_store.reshape(DB, 2 * H), down_store.reshape(H, DB),
    )
    return pl.pallas_call(
        restore,
        out_shape=jax.ShapeDtypeStruct((TOK, D), BF),
        in_specs=[pl.BlockSpec(memory_space=pltpu.SMEM), vmem],
        out_specs=vmem,
        compiler_params=pltpu.CompilerParams(vmem_limit_bytes=4 << 20),
        name="restore",
    )(held_bucket, mixed)


def solution(mesh):
    in_specs = (
        P(("rep", "exp"), None),
        P(("rep", "exp"), None),
        P(("rep", "exp"), None),
        P("exp", "rep", None),
        P("exp", None, "rep"),
        P(),
    )
    out_specs = P(("rep", "exp"), None)
    return jax.shard_map(local, mesh=mesh, in_specs=in_specs, out_specs=out_specs, check_vma=False)
```

```python
import functools

import jax
import jax.numpy as jnp
from jax import lax
from jax.experimental import pallas as pl
from jax.experimental.pallas import tpu as pltpu
from jax.sharding import PartitionSpec as P

MESH = pl.DeviceIdType.MESH
D = 2048
H = 768
TOK = 128
DB = 128
NR = 16
PK = 16
PW = 1536
SLOTS = 32
ROWS = SLOTS * PK
STEPS = (4, 3, -3, 2, -2, 1, -1, 0)
GROUPS = ((0, 12), (12, 20), (20, 32))
MIX = ((0, 16), (16, 32))
SELF = 28
CH = 3
BF = jnp.bfloat16
F32 = jnp.float32


def dot(a, b):
    return jnp.dot(a, b, preferred_element_type=F32)


def kernel(
    held, tok_in, routes_in, weight_in, gu, dn, out,
    gu_all, dn_all, tperm, opk, rcv, ppk, ret, wmix, xbuf, hid, p3, phi, comb,
    tok, routes, weight, inp, loc, zs, zr, xs, xr, cs, cr, ds, dr, rs, rr,
):
    rep = lax.axis_index("rep")
    ex = lax.axis_index("exp")
    c = rep % 2
    x = (rep // 2) % 4
    zh = rep // 8
    y = ex // 8
    z = zh * 8 + ex % 8

    def dev(ax, ay, az, ac):
        ax = (ax + 4) % 4
        ay = (ay + 4) % 4
        az = (az + 16) % 16
        return (((az // 8) * 4 + ax) * 2 + ac, ay * 8 + az % 8)

    def owner(azh, ax, ac):
        return (azh * 4 + (ax + 4) % 4) * 2 + ac

    def disp(k):
        return 4 - 8 * c if STEPS[k] == 4 else STEPS[k]

    loads = [
        pltpu.make_async_copy(a, b, inp.at[i])
        for i, (a, b) in enumerate(((tok_in, tok), (routes_in, routes), (weight_in, weight)))
    ]
    for cp in loads:
        cp.start()

    partners = [dev(x, y, z + 8, c), dev(x, y, z, 1 - c)]
    partners += [dev(x + k, y, z, c) for k in (1, 2, 3)]
    for d in range(-4, 5):
        for dy in range(4):
            if d or dy:
                partners.append(dev(x, y + dy, z + d, c))
    barrier = pltpu.get_barrier_semaphore()
    for p in partners:
        pl.semaphore_signal(barrier, inc=1, device_id=p, device_id_type=MESH)
    pl.semaphore_wait(barrier, len(partners))

    mine = owner(zh, x, c)
    far = owner(1 - zh, x, c)

    def own(ch):
        return dn if ch == 2 else gu.at[pl.ds(64 * ch, 64)]

    def slot(r, ch):
        if ch == 2:
            return dn_all.at[r]
        return gu_all.at[pl.ds(pl.multiple_of(r * DB + 64 * ch, 64), 64)]

    def send(src, dst, ss, rsem, to):
        return pltpu.make_async_remote_copy(
            src_ref=src, dst_ref=dst, send_sem=ss, recv_sem=rsem,
            device_id=to, device_id_type=MESH,
        )

    started = []

    def go(cp):
        cp.start()
        started.append(cp)

    def arrived(dst, ss, rsem, to):
        send(dst, dst, ss, rsem, to).wait_recv()

    core = dev(x, y, z, 1 - c)
    for ch in range(CH):
        go(send(own(ch), slot(mine, ch), zs.at[ch], zr.at[ch], dev(x, y, z + 8, c)))
    for ch in range(CH):
        for k in (1, 3, 2):
            i = ch * 3 + k - 1
            go(send(own(ch), slot(mine, ch), xs.at[i], xr.at[i], dev(x + k, y, z, c)))
    for ch in range(CH):
        go(send(own(ch), slot(mine, ch), cs.at[ch], cr.at[ch], core))
    keep = [pltpu.make_async_copy(own(ch), slot(mine, ch), loc.at[ch]) for ch in range(CH)]
    for cp in keep:
        cp.start()

    for cp in loads:
        cp.wait()

    for r in range(NR):
        pick = tok[:, 0:DB]
        for b in range(1, NR):
            pick = jnp.where(held[r] == b, tok[:, b * DB : (b + 1) * DB], pick)
        tperm[:, r * DB : (r + 1) * DB] = pick

    lane = lax.broadcasted_iota(jnp.int32, (TOK, 128), 1)
    row = lax.broadcasted_iota(jnp.int32, (TOK, 128), 0)
    lower = (lane < row).astype(F32).astype(BF)

    def column(v):
        return jnp.transpose(jnp.broadcast_to(v, (128, TOK)))

    named = [column(routes[k : k + 1, :].astype(F32)) for k in range(2)]
    share = [column(weight[k : k + 1, :]) for k in range(2)]
    hot0 = (lane.astype(F32) == named[0]).astype(F32)
    hot1 = (lane.astype(F32) == named[1]).astype(F32)
    seen0 = dot(lower, hot0.astype(BF))
    seen1 = dot(lower, hot1.astype(BF)) + jnp.sum(hot0, axis=0, keepdims=True)
    dz = (lane % 8 - ex % 8 + 8) % 8
    step = jnp.where(dz < 4, 7 - 2 * dz, 2 * dz - 8)
    place = (step * 4 + (lane // 8 - y + 16) % 4).astype(F32)
    wide = lax.broadcasted_iota(jnp.int32, (TOK, ROWS), 1).astype(F32)
    tall = row.astype(F32)
    keys = []
    for hot, seen in ((hot0, seen0), (hot1, seen1)):
        base = jnp.sum(hot * place, axis=1, keepdims=True) * PK
        rank = jnp.sum(hot * seen, axis=1, keepdims=True)
        quad = (rank >= 4.0).astype(F32) + (rank >= 8.0).astype(F32)
        keys.append((base + rank, base + 12.0 + rank - 4.0 * quad, quad))
    for j in range(4):
        mix = jnp.zeros((TOK, ROWS), F32)
        for k, (lo, hi, quad) in enumerate(keys):
            key = lo if j == 3 else jnp.where(quad == float(j), hi, -1.0)
            mix = mix + jnp.where(wide == key, share[k][:, 0:1], 0.0)
        top = mix.astype(BF)
        wmix[j, 0:TOK, :] = top
        wmix[j, TOK : 2 * TOK, :] = (mix - top.astype(F32)).astype(BF)
    turned = []
    for lo, hi, quad in keys:
        turned.append(
            tuple(jnp.transpose(jnp.broadcast_to(v, (TOK, 128))) for v in (lo, hi, quad))
        )
    for b in range(ROWS // 128):
        at = tall + float(b * 128)
        low = jnp.zeros((128, TOK), F32)
        for lo, hi, quad in turned:
            low = low + (at == lo).astype(F32)
        for j in range(3):
            high = jnp.zeros((128, TOK), F32)
            for lo, hi, quad in turned:
                high = high + (at == jnp.where(quad == float(j), hi, -1.0)).astype(F32)
            block = dot(low.astype(BF), tperm[:, 512 * j : 512 * (j + 1)])
            block = block + dot(high.astype(BF), tperm[:, PW:D])
            opk[b * 128 : (b + 1) * 128, 512 * j : 512 * (j + 1)] = block.astype(BF)

    def tile(ref, i):
        return ref.at[pl.ds(i * PK, PK)]

    def dispatch(first, last):
        for i in range(first, last):
            if i == SELF:
                continue
            k, dy = i // 4, i % 4
            go(send(
                tile(opk, i), tile(rcv, i), ds.at[i], dr.at[i],
                dev(x, y + dy, z + disp(k), c),
            ))

    def from_x(ch, part):
        for k in (1, 3, 2):
            i = part * 9 + ch * 3 + k - 1
            r = owner(zh if part == 0 else 1 - zh, x - k, c)
            arrived(slot(r, ch), xs.at[i], xr.at[i], dev(x + k, y, z, c))
            n = 6 + i
            go(send(slot(r, ch), slot(r, ch), cs.at[n], cr.at[n], core))

    for ch in range(CH):
        from_x(ch, 0)
        arrived(slot(far, ch), zs.at[ch], zr.at[ch], dev(x, y, z + 8, c))
        for k in (1, 3, 2):
            i = 9 + ch * 3 + k - 1
            go(send(slot(far, ch), slot(far, ch), xs.at[i], xr.at[i], dev(x + k, y, z, c)))
        go(send(slot(far, ch), slot(far, ch), cs.at[3 + ch], cr.at[3 + ch], core))
        if ch == 1:
            dispatch(0, SLOTS)
            rcv[SELF * PK : (SELF + 1) * PK, :] = opk[SELF * PK : (SELF + 1) * PK, :]
    for ch in range(CH):
        from_x(ch, 1)
    for ch in range(CH):
        arrived(slot(owner(zh, x, 1 - c), ch), cs.at[ch], cr.at[ch], core)
        arrived(slot(owner(1 - zh, x, 1 - c), ch), cs.at[3 + ch], cr.at[3 + ch], core)
        for part in range(2):
            for k in (1, 2, 3):
                n = 6 + part * 9 + ch * 3 + k - 1
                r = owner(zh if part == 0 else 1 - zh, x - k, 1 - c)
                arrived(slot(r, ch), cs.at[n], cr.at[n], core)
    for cp in keep:
        cp.wait()

    for first, last in GROUPS:
        n = (last - first) * PK
        lo = first * PK
        for i in range(first, last):
            if i == SELF:
                continue
            k, dy = i // 4, i % 4
            arrived(tile(rcv, i), ds.at[i], dr.at[i], dev(x, y + dy, z + disp(k), c))
        a = lax.broadcasted_iota(jnp.int32, (n, n), 0)
        b = lax.broadcasted_iota(jnp.int32, (n, n), 1)
        same = (a // PK) == (b // PK)
        ai, bi = a % PK, b % PK
        xbuf[0:n, 0:PW] = rcv[lo : lo + n, :]
        tail = jnp.zeros((n, 512), F32)
        for j in range(3):
            take = same & (ai // 4 == j) & (bi == 12 + ai % 4)
            tail = tail + dot(
                take.astype(F32).astype(BF), rcv[lo : lo + n, 512 * j : 512 * (j + 1)]
            )
        xbuf[0:n, PW:D] = tail.astype(BF)

        def up(t, carry):
            col = pl.multiple_of(t * 256, 256)
            g = dot(xbuf[0:n, :], gu_all[:, pl.ds(col, 256)])
            u = dot(xbuf[0:n, :], gu_all[:, pl.ds(pl.multiple_of(H + col, 256), 256)])
            hid[0:n, pl.ds(col, 256)] = (g / (1.0 + jnp.exp(-g)) * u).astype(BF)
            return carry

        lax.fori_loop(0, 3, up, 0)

        def down(q):
            w = jnp.concatenate([dn_all[2 * q], dn_all[2 * q + 1]], axis=1)
            return dot(hid[0:n, :], w).astype(BF)

        for q in (6, 7):
            p3[0:n, (q - 6) * 256 : (q - 5) * 256] = down(q)
        for j in range(3):
            put = same & (bi // 4 == j) & (ai == 12 + bi % 4)
            phi[0:n, 512 * j : 512 * (j + 1)] = dot(
                put.astype(F32).astype(BF), p3[0:n, :]
            ).astype(BF)
        real = lax.broadcasted_iota(jnp.int32, (n, 256), 0) % PK < 12

        def pack(q, carry):
            col = pl.multiple_of(q * 256, 256)
            v = jnp.where(real, down(q).astype(F32), phi[0:n, pl.ds(col, 256)].astype(F32))
            ppk[lo : lo + n, pl.ds(col, 256)] = v.astype(BF)
            return carry

        lax.fori_loop(0, 6, pack, 0)
        for i in range(first, last):
            if i == SELF:
                continue
            k, dy = i // 4, i % 4
            go(send(
                tile(ppk, i), tile(ret, i), rs.at[i], rr.at[i],
                dev(x, y - dy, z - disp(k), c),
            ))
    ret[SELF * PK : (SELF + 1) * PK, :] = ppk[SELF * PK : (SELF + 1) * PK, :]

    def put(first, cols, m):
        v = m[0:TOK] + m[TOK : 2 * TOK]
        if first == 0:
            comb[:, cols] = v
        else:
            out[:, cols] = (comb[:, cols] + v).astype(BF)

    for first, last in MIX:
        for i in range(first, last):
            if i == SELF:
                continue
            k, dy = i // 4, i % 4
            arrived(tile(ret, i), rs.at[i], rr.at[i], dev(x, y - dy, z - disp(k), c))
        lo, hi = first * PK, last * PK
        part = jnp.zeros((2 * TOK, 512), F32)
        for j in range(3):
            block = ret[lo:hi, 512 * j : 512 * (j + 1)]
            m = dot(wmix[3, :, lo:hi], block)
            part = part + dot(wmix[j, :, lo:hi], block)
            put(first, slice(512 * j, 512 * (j + 1)), m)
        put(first, slice(PW, D), part)

    for cp in started:
        cp.wait_send()


def restore(held, mixed, out):
    for r in range(NR):
        col = pl.multiple_of(held[r] * DB, DB)
        out[:, pl.ds(col, DB)] = mixed[:, r * DB : (r + 1) * DB]


def local(tokens, routes, route_weight, gate_up_store, down_store, held_bucket):
    vmem = pl.BlockSpec(memory_space=pltpu.VMEM)
    dma = pltpu.SemaphoreType.DMA
    most = max(b - a for a, b in GROUPS) * PK
    mixed = pl.pallas_call(
        kernel,
        out_shape=jax.ShapeDtypeStruct((TOK, D), BF),
        in_specs=[pl.BlockSpec(memory_space=pltpu.SMEM)]
        + [pl.BlockSpec(memory_space=pltpu.HBM)] * 5,
        out_specs=vmem,
        scratch_shapes=[
            pltpu.VMEM((D, 2 * H), BF),
            pltpu.VMEM((NR, H, DB), BF),
            pltpu.VMEM((TOK, D), BF),
            pltpu.VMEM((ROWS, PW), BF),
            pltpu.VMEM((ROWS, PW), BF),
            pltpu.VMEM((ROWS, PW), BF),
            pltpu.VMEM((ROWS, PW), BF),
            pltpu.VMEM((4, 2 * TOK, ROWS), BF),
            pltpu.VMEM((most, D), BF),
            pltpu.VMEM((most, H), BF),
            pltpu.VMEM((most, 512), BF),
            pltpu.VMEM((most, PW), BF),
            pltpu.VMEM((TOK, D), F32),
            pltpu.VMEM((TOK, D), BF),
            pltpu.VMEM((2, TOK), jnp.int32),
            pltpu.VMEM((2, TOK), F32),
            dma((3,)),
            dma((CH,)),
            dma((CH,)), dma((CH,)),
            dma((18,)), dma((18,)),
            dma((24,)), dma((24,)),
            dma((SLOTS,)), dma((SLOTS,)),
            dma((SLOTS,)), dma((SLOTS,)),
        ],
        compiler_params=pltpu.CompilerParams(
            collective_id=0, has_side_effects=True, vmem_limit_bytes=60 << 20
        ),
        name="layer",
    )(
        held_bucket, tokens, routes.T, route_weight.T,
        gate_up_store.reshape(DB, 2 * H), down_store.reshape(H, DB),
    )
    return pl.pallas_call(
        restore,
        out_shape=jax.ShapeDtypeStruct((TOK, D), BF),
        in_specs=[pl.BlockSpec(memory_space=pltpu.SMEM), vmem],
        out_specs=vmem,
        name="restore",
    )(held_bucket, mixed)


def solution(mesh):
    in_specs = (
        P(("rep", "exp"), None),
        P(("rep", "exp"), None),
        P(("rep", "exp"), None),
        P("exp", "rep", None),
        P("exp", None, "rep"),
        P(),
    )
    out_specs = P(("rep", "exp"), None)
    return jax.shard_map(local, mesh=mesh, in_specs=in_specs, out_specs=out_specs, check_vma=False)
```

```python
import functools

import jax
import jax.numpy as jnp
from jax import lax
from jax.experimental import pallas as pl
from jax.experimental.pallas import tpu as pltpu
from jax.sharding import PartitionSpec as P

MESH = pl.DeviceIdType.MESH
D = 2048
H = 768
TOK = 128
DB = 128
NR = 16
PK = 16
PW = 1536
SLOTS = 32
ROWS = SLOTS * PK
STEPS = (4, 3, -3, 2, -2, 1, -1, 0)
GROUPS = ((0, 12), (12, 20), (20, 32))
MIX = ((0, 16), (16, 32))
SELF = 28
CH = 3
BF = jnp.bfloat16
F32 = jnp.float32


def dot(a, b):
    return jnp.dot(a, b, preferred_element_type=F32)


def kernel(
    held, tok_in, routes_in, weight_in, gu, dn, out,
    gu_all, dn_all, tperm, opk, rcv, ppk, ret, wmix, xbuf, hid, p3, phi, comb,
    tok, routes, weight, inp, loc, zs, zr, xs, xr, cs, cr, ds, dr, rs, rr,
):
    rep = lax.axis_index("rep")
    ex = lax.axis_index("exp")
    c = rep % 2
    x = (rep // 2) % 4
    zh = rep // 8
    y = ex // 8
    z = zh * 8 + ex % 8

    def dev(ax, ay, az, ac):
        ax = (ax + 4) % 4
        ay = (ay + 4) % 4
        az = (az + 16) % 16
        return (((az // 8) * 4 + ax) * 2 + ac, ay * 8 + az % 8)

    def owner(azh, ax, ac):
        return (azh * 4 + (ax + 4) % 4) * 2 + ac

    def disp(k):
        return 4 - 8 * c if STEPS[k] == 4 else STEPS[k]

    loads = [
        pltpu.make_async_copy(a, b, inp.at[i])
        for i, (a, b) in enumerate(((tok_in, tok), (routes_in, routes), (weight_in, weight)))
    ]
    for cp in loads:
        cp.start()

    partners = [dev(x, y, z + 8, c), dev(x, y, z, 1 - c)]
    partners += [dev(x + k, y, z, c) for k in (1, 2, 3)]
    for d in range(-4, 5):
        for dy in range(4):
            if d or dy:
                partners.append(dev(x, y + dy, z + d, c))
    barrier = pltpu.get_barrier_semaphore()
    for p in partners:
        pl.semaphore_signal(barrier, inc=1, device_id=p, device_id_type=MESH)
    pl.semaphore_wait(barrier, len(partners))

    mine = owner(zh, x, c)
    far = owner(1 - zh, x, c)

    def own(ch):
        return dn if ch == 2 else gu.at[pl.ds(64 * ch, 64)]

    def slot(r, ch):
        if ch == 2:
            return dn_all.at[r]
        return gu_all.at[pl.ds(pl.multiple_of(r * DB + 64 * ch, 64), 64)]

    def send(src, dst, ss, rsem, to):
        return pltpu.make_async_remote_copy(
            src_ref=src, dst_ref=dst, send_sem=ss, recv_sem=rsem,
            device_id=to, device_id_type=MESH,
        )

    started = []

    def go(cp):
        cp.start()
        started.append(cp)

    def arrived(dst, ss, rsem, to):
        send(dst, dst, ss, rsem, to).wait_recv()

    core = dev(x, y, z, 1 - c)
    for ch in range(CH):
        go(send(own(ch), slot(mine, ch), zs.at[ch], zr.at[ch], dev(x, y, z + 8, c)))
    for ch in range(CH):
        for k in (1, 3, 2):
            i = ch * 3 + k - 1
            go(send(own(ch), slot(mine, ch), xs.at[i], xr.at[i], dev(x + k, y, z, c)))
    for ch in range(CH):
        go(send(own(ch), slot(mine, ch), cs.at[ch], cr.at[ch], core))
    keep = [pltpu.make_async_copy(own(ch), slot(mine, ch), loc.at[ch]) for ch in range(CH)]
    for cp in keep:
        cp.start()

    for cp in loads:
        cp.wait()

    for r in range(NR):
        pick = tok[:, 0:DB]
        for b in range(1, NR):
            pick = jnp.where(held[r] == b, tok[:, b * DB : (b + 1) * DB], pick)
        tperm[:, r * DB : (r + 1) * DB] = pick

    lane = lax.broadcasted_iota(jnp.int32, (TOK, 128), 1)
    row = lax.broadcasted_iota(jnp.int32, (TOK, 128), 0)
    lower = (lane < row).astype(F32).astype(BF)

    def column(v):
        return jnp.transpose(jnp.broadcast_to(v, (128, TOK)))

    named = [column(routes[k : k + 1, :].astype(F32)) for k in range(2)]
    share = [column(weight[k : k + 1, :]) for k in range(2)]
    hot0 = (lane.astype(F32) == named[0]).astype(F32)
    hot1 = (lane.astype(F32) == named[1]).astype(F32)
    seen0 = dot(lower, hot0.astype(BF))
    seen1 = dot(lower, hot1.astype(BF)) + jnp.sum(hot0, axis=0, keepdims=True)
    dz = (lane % 8 - ex % 8 + 8) % 8
    step = jnp.where(dz < 4, 7 - 2 * dz, 2 * dz - 8)
    place = (step * 4 + (lane // 8 - y + 16) % 4).astype(F32)
    wide = lax.broadcasted_iota(jnp.int32, (TOK, ROWS), 1).astype(F32)
    tall = row.astype(F32)
    keys = []
    for hot, seen in ((hot0, seen0), (hot1, seen1)):
        base = jnp.sum(hot * place, axis=1, keepdims=True) * PK
        rank = jnp.sum(hot * seen, axis=1, keepdims=True)
        quad = (rank >= 4.0).astype(F32) + (rank >= 8.0).astype(F32)
        keys.append((base + rank, base + 12.0 + rank - 4.0 * quad, quad))
    for j in range(4):
        mix = jnp.zeros((TOK, ROWS), F32)
        for k, (lo, hi, quad) in enumerate(keys):
            key = lo if j == 3 else jnp.where(quad == float(j), hi, -1.0)
            mix = mix + jnp.where(wide == key, share[k][:, 0:1], 0.0)
        top = mix.astype(BF)
        wmix[j, 0:TOK, :] = top
        wmix[j, TOK : 2 * TOK, :] = (mix - top.astype(F32)).astype(BF)
    turned = []
    for lo, hi, quad in keys:
        turned.append(
            tuple(jnp.transpose(jnp.broadcast_to(v, (TOK, 128))) for v in (lo, hi, quad))
        )
    for b in range(ROWS // 128):
        at = tall + float(b * 128)
        low = jnp.zeros((128, TOK), F32)
        for lo, hi, quad in turned:
            low = low + (at == lo).astype(F32)
        for j in range(3):
            high = jnp.zeros((128, TOK), F32)
            for lo, hi, quad in turned:
                high = high + (at == jnp.where(quad == float(j), hi, -1.0)).astype(F32)
            block = dot(low.astype(BF), tperm[:, 512 * j : 512 * (j + 1)])
            block = block + dot(high.astype(BF), tperm[:, PW:D])
            opk[b * 128 : (b + 1) * 128, 512 * j : 512 * (j + 1)] = block.astype(BF)

    def tile(ref, i):
        return ref.at[pl.ds(i * PK, PK)]

    def dispatch(first, last):
        for i in range(first, last):
            if i == SELF:
                continue
            k, dy = i // 4, i % 4
            go(send(
                tile(opk, i), tile(rcv, i), ds.at[i], dr.at[i],
                dev(x, y + dy, z + disp(k), c),
            ))

    def from_x(ch, part):
        for k in (1, 3, 2):
            i = part * 9 + ch * 3 + k - 1
            r = owner(zh if part == 0 else 1 - zh, x - k, c)
            arrived(slot(r, ch), xs.at[i], xr.at[i], dev(x + k, y, z, c))
            n = 6 + i
            go(send(slot(r, ch), slot(r, ch), cs.at[n], cr.at[n], core))

    for ch in range(CH):
        from_x(ch, 0)
        arrived(slot(far, ch), zs.at[ch], zr.at[ch], dev(x, y, z + 8, c))
        for k in (1, 3, 2):
            i = 9 + ch * 3 + k - 1
            go(send(slot(far, ch), slot(far, ch), xs.at[i], xr.at[i], dev(x + k, y, z, c)))
        go(send(slot(far, ch), slot(far, ch), cs.at[3 + ch], cr.at[3 + ch], core))
        if ch == 1:
            dispatch(0, SLOTS)
            rcv[SELF * PK : (SELF + 1) * PK, :] = opk[SELF * PK : (SELF + 1) * PK, :]
    for ch in range(CH):
        from_x(ch, 1)
    for ch in range(CH):
        arrived(slot(owner(zh, x, 1 - c), ch), cs.at[ch], cr.at[ch], core)
        arrived(slot(owner(1 - zh, x, 1 - c), ch), cs.at[3 + ch], cr.at[3 + ch], core)
        for part in range(2):
            for k in (1, 2, 3):
                n = 6 + part * 9 + ch * 3 + k - 1
                r = owner(zh if part == 0 else 1 - zh, x - k, 1 - c)
                arrived(slot(r, ch), cs.at[n], cr.at[n], core)
    for cp in keep:
        cp.wait()

    for first, last in GROUPS:
        n = (last - first) * PK
        lo = first * PK
        for i in range(first, last):
            if i == SELF:
                continue
            k, dy = i // 4, i % 4
            arrived(tile(rcv, i), ds.at[i], dr.at[i], dev(x, y + dy, z + disp(k), c))
        a = lax.broadcasted_iota(jnp.int32, (n, n), 0)
        b = lax.broadcasted_iota(jnp.int32, (n, n), 1)
        same = (a // PK) == (b // PK)
        ai, bi = a % PK, b % PK
        xbuf[0:n, 0:PW] = rcv[lo : lo + n, :]
        tail = jnp.zeros((n, 512), F32)
        for j in range(3):
            take = same & (ai // 4 == j) & (bi == 12 + ai % 4)
            tail = tail + dot(
                take.astype(F32).astype(BF), rcv[lo : lo + n, 512 * j : 512 * (j + 1)]
            )
        xbuf[0:n, PW:D] = tail.astype(BF)

        def up(t, carry):
            col = pl.multiple_of(t * 256, 256)
            g = dot(xbuf[0:n, :], gu_all[:, pl.ds(col, 256)])
            u = dot(xbuf[0:n, :], gu_all[:, pl.ds(pl.multiple_of(H + col, 256), 256)])
            hid[0:n, pl.ds(col, 256)] = (g / (1.0 + jnp.exp(-g)) * u).astype(BF)
            return carry

        lax.fori_loop(0, 3, up, 0)

        def down(q):
            w = jnp.concatenate([dn_all[2 * q], dn_all[2 * q + 1]], axis=1)
            return dot(hid[0:n, :], w).astype(BF)

        for q in (6, 7):
            p3[0:n, (q - 6) * 256 : (q - 5) * 256] = down(q)
        for j in range(3):
            put = same & (bi // 4 == j) & (ai == 12 + bi % 4)
            phi[0:n, 512 * j : 512 * (j + 1)] = dot(
                put.astype(F32).astype(BF), p3[0:n, :]
            ).astype(BF)
        real = lax.broadcasted_iota(jnp.int32, (n, 256), 0) % PK < 12

        def pack(q, carry):
            col = pl.multiple_of(q * 256, 256)
            v = jnp.where(real, down(q).astype(F32), phi[0:n, pl.ds(col, 256)].astype(F32))
            ppk[lo : lo + n, pl.ds(col, 256)] = v.astype(BF)
            return carry

        lax.fori_loop(0, 6, pack, 0)
        for i in range(first, last):
            if i == SELF:
                continue
            k, dy = i // 4, i % 4
            go(send(
                tile(ppk, i), tile(ret, i), rs.at[i], rr.at[i],
                dev(x, y - dy, z - disp(k), c),
            ))
    ret[SELF * PK : (SELF + 1) * PK, :] = ppk[SELF * PK : (SELF + 1) * PK, :]

    def put(first, cols, m):
        v = m[0:TOK] + m[TOK : 2 * TOK]
        if first == 0:
            comb[:, cols] = v
        else:
            out[:, cols] = (comb[:, cols] + v).astype(BF)

    for first, last in MIX:
        for i in range(first, last):
            if i == SELF:
                continue
            k, dy = i // 4, i % 4
            arrived(tile(ret, i), rs.at[i], rr.at[i], dev(x, y - dy, z - disp(k), c))
        lo, hi = first * PK, last * PK
        part = jnp.zeros((2 * TOK, 512), F32)
        for j in range(3):
            block = ret[lo:hi, 512 * j : 512 * (j + 1)]
            m = dot(wmix[3, :, lo:hi], block)
            part = part + dot(wmix[j, :, lo:hi], block)
            put(first, slice(512 * j, 512 * (j + 1)), m)
        put(first, slice(PW, D), part)

    for cp in started:
        cp.wait_send()


def restore(held, mixed, out, sems):
    copies = []
    for r in range(NR):
        col = pl.multiple_of(held[r] * DB, DB)
        copies.append(pltpu.make_async_copy(
            mixed.at[:, pl.ds(r * DB, DB)], out.at[:, pl.ds(col, DB)], sems.at[r]
        ))
        copies[-1].start()
    for cp in copies:
        cp.wait()


def local(tokens, routes, route_weight, gate_up_store, down_store, held_bucket):
    vmem = pl.BlockSpec(memory_space=pltpu.VMEM)
    dma = pltpu.SemaphoreType.DMA
    most = max(b - a for a, b in GROUPS) * PK
    mixed = pl.pallas_call(
        kernel,
        out_shape=jax.ShapeDtypeStruct((TOK, D), BF),
        in_specs=[pl.BlockSpec(memory_space=pltpu.SMEM)]
        + [pl.BlockSpec(memory_space=pltpu.HBM)] * 5,
        out_specs=vmem,
        scratch_shapes=[
            pltpu.VMEM((D, 2 * H), BF),
            pltpu.VMEM((NR, H, DB), BF),
            pltpu.VMEM((TOK, D), BF),
            pltpu.VMEM((ROWS, PW), BF),
            pltpu.VMEM((ROWS, PW), BF),
            pltpu.VMEM((ROWS, PW), BF),
            pltpu.VMEM((ROWS, PW), BF),
            pltpu.VMEM((4, 2 * TOK, ROWS), BF),
            pltpu.VMEM((most, D), BF),
            pltpu.VMEM((most, H), BF),
            pltpu.VMEM((most, 512), BF),
            pltpu.VMEM((most, PW), BF),
            pltpu.VMEM((TOK, D), F32),
            pltpu.VMEM((TOK, D), BF),
            pltpu.VMEM((2, TOK), jnp.int32),
            pltpu.VMEM((2, TOK), F32),
            dma((3,)),
            dma((CH,)),
            dma((CH,)), dma((CH,)),
            dma((18,)), dma((18,)),
            dma((24,)), dma((24,)),
            dma((SLOTS,)), dma((SLOTS,)),
            dma((SLOTS,)), dma((SLOTS,)),
        ],
        compiler_params=pltpu.CompilerParams(
            collective_id=0, has_side_effects=True, vmem_limit_bytes=60 << 20
        ),
        name="layer",
    )(
        held_bucket, tokens, routes.T, route_weight.T,
        gate_up_store.reshape(DB, 2 * H), down_store.reshape(H, DB),
    )
    return pl.pallas_call(
        restore,
        out_shape=jax.ShapeDtypeStruct((TOK, D), BF),
        in_specs=[pl.BlockSpec(memory_space=pltpu.SMEM), pl.BlockSpec(memory_space=pltpu.HBM)],
        out_specs=pl.BlockSpec(memory_space=pltpu.HBM),
        scratch_shapes=[dma((NR,))],
        name="restore",
    )(held_bucket, mixed)


def solution(mesh):
    in_specs = (
        P(("rep", "exp"), None),
        P(("rep", "exp"), None),
        P(("rep", "exp"), None),
        P("exp", "rep", None),
        P("exp", None, "rep"),
        P(),
    )
    out_specs = P(("rep", "exp"), None)
    return jax.shard_map(local, mesh=mesh, in_specs=in_specs, out_specs=out_specs, check_vma=False)
```

```python
import functools

import jax
import jax.numpy as jnp
from jax import lax
from jax.experimental import pallas as pl
from jax.experimental.pallas import tpu as pltpu
from jax.sharding import PartitionSpec as P

MESH = pl.DeviceIdType.MESH
D = 2048
H = 768
TOK = 128
DB = 128
NR = 16
PK = 16
PW = 1536
SLOTS = 32
ROWS = SLOTS * PK
STEPS = (4, 3, -3, 2, -2, 1, -1, 0)
GROUPS = ((0, 12), (12, 20), (20, 32))
MIX = ((0, 16), (16, 32))
SELF = 28
CH = 3
BF = jnp.bfloat16
F32 = jnp.float32


def dot(a, b):
    return jnp.dot(a, b, preferred_element_type=F32)


def kernel(
    held, tok_in, routes_in, weight_in, gu, dn, out,
    gu_all, dn_all, tperm, opk, rcv, ppk, ret, wmix, xbuf, hid, p3, phi, comb,
    tok, routes, weight, inp, loc, zs, zr, xs, xr, cs, cr, ds, dr, rs, rr,
):
    rep = lax.axis_index("rep")
    ex = lax.axis_index("exp")
    c = rep % 2
    x = (rep // 2) % 4
    zh = rep // 8
    y = ex // 8
    z = zh * 8 + ex % 8

    def dev(ax, ay, az, ac):
        ax = (ax + 4) % 4
        ay = (ay + 4) % 4
        az = (az + 16) % 16
        return (((az // 8) * 4 + ax) * 2 + ac, ay * 8 + az % 8)

    def owner(azh, ax, ac):
        return (azh * 4 + (ax + 4) % 4) * 2 + ac

    def disp(k):
        return 4 - 8 * c if STEPS[k] == 4 else STEPS[k]

    loads = [
        pltpu.make_async_copy(a, b, inp.at[i])
        for i, (a, b) in enumerate(((tok_in, tok), (routes_in, routes), (weight_in, weight)))
    ]
    for cp in loads:
        cp.start()

    partners = [dev(x, y, z + 8, c), dev(x, y, z, 1 - c)]
    partners += [dev(x + k, y, z, c) for k in (1, 2, 3)]
    for d in range(-4, 5):
        for dy in range(4):
            if d or dy:
                partners.append(dev(x, y + dy, z + d, c))
    barrier = pltpu.get_barrier_semaphore()
    for p in partners:
        pl.semaphore_signal(barrier, inc=1, device_id=p, device_id_type=MESH)
    pl.semaphore_wait(barrier, len(partners))

    mine = owner(zh, x, c)
    far = owner(1 - zh, x, c)

    def own(ch):
        return dn if ch == 2 else gu.at[pl.ds(64 * ch, 64)]

    def slot(r, ch):
        if ch == 2:
            return dn_all.at[r]
        return gu_all.at[pl.ds(pl.multiple_of(r * DB + 64 * ch, 64), 64)]

    def send(src, dst, ss, rsem, to):
        return pltpu.make_async_remote_copy(
            src_ref=src, dst_ref=dst, send_sem=ss, recv_sem=rsem,
            device_id=to, device_id_type=MESH,
        )

    started = []

    def go(cp):
        cp.start()
        started.append(cp)

    def arrived(dst, ss, rsem, to):
        send(dst, dst, ss, rsem, to).wait_recv()

    core = dev(x, y, z, 1 - c)
    for ch in range(CH):
        go(send(own(ch), slot(mine, ch), zs.at[ch], zr.at[ch], dev(x, y, z + 8, c)))
    for ch in range(CH):
        for k in (1, 3, 2):
            i = ch * 3 + k - 1
            go(send(own(ch), slot(mine, ch), xs.at[i], xr.at[i], dev(x + k, y, z, c)))
    for ch in range(CH):
        go(send(own(ch), slot(mine, ch), cs.at[ch], cr.at[ch], core))
    keep = [pltpu.make_async_copy(own(ch), slot(mine, ch), loc.at[ch]) for ch in range(CH)]
    for cp in keep:
        cp.start()

    for cp in loads:
        cp.wait()

    for r in range(NR):
        pick = tok[:, 0:DB]
        for b in range(1, NR):
            pick = jnp.where(held[r] == b, tok[:, b * DB : (b + 1) * DB], pick)
        tperm[:, r * DB : (r + 1) * DB] = pick

    lane = lax.broadcasted_iota(jnp.int32, (TOK, 128), 1)
    row = lax.broadcasted_iota(jnp.int32, (TOK, 128), 0)
    lower = (lane < row).astype(F32).astype(BF)

    def column(v):
        return jnp.transpose(jnp.broadcast_to(v, (128, TOK)))

    named = [column(routes[k : k + 1, :].astype(F32)) for k in range(2)]
    share = [column(weight[k : k + 1, :]) for k in range(2)]
    hot0 = (lane.astype(F32) == named[0]).astype(F32)
    hot1 = (lane.astype(F32) == named[1]).astype(F32)
    seen0 = dot(lower, hot0.astype(BF))
    seen1 = dot(lower, hot1.astype(BF)) + jnp.sum(hot0, axis=0, keepdims=True)
    dz = (lane % 8 - ex % 8 + 8) % 8
    step = jnp.where(dz < 4, 7 - 2 * dz, 2 * dz - 8)
    place = (step * 4 + (lane // 8 - y + 16) % 4).astype(F32)
    wide = lax.broadcasted_iota(jnp.int32, (TOK, ROWS), 1).astype(F32)
    tall = row.astype(F32)
    keys = []
    for hot, seen in ((hot0, seen0), (hot1, seen1)):
        base = jnp.sum(hot * place, axis=1, keepdims=True) * PK
        rank = jnp.sum(hot * seen, axis=1, keepdims=True)
        quad = (rank >= 4.0).astype(F32) + (rank >= 8.0).astype(F32)
        keys.append((base + rank, base + 12.0 + rank - 4.0 * quad, quad))
    for j in range(4):
        mix = jnp.zeros((TOK, ROWS), F32)
        for k, (lo, hi, quad) in enumerate(keys):
            key = lo if j == 3 else jnp.where(quad == float(j), hi, -1.0)
            mix = mix + jnp.where(wide == key, share[k][:, 0:1], 0.0)
        top = mix.astype(BF)
        wmix[j, 0:TOK, :] = top
        wmix[j, TOK : 2 * TOK, :] = (mix - top.astype(F32)).astype(BF)
    turned = []
    for lo, hi, quad in keys:
        turned.append(
            tuple(jnp.transpose(jnp.broadcast_to(v, (TOK, 128))) for v in (lo, hi, quad))
        )
    for b in range(ROWS // 128):
        at = tall + float(b * 128)
        low = jnp.zeros((128, TOK), F32)
        for lo, hi, quad in turned:
            low = low + (at == lo).astype(F32)
        for j in range(3):
            high = jnp.zeros((128, TOK), F32)
            for lo, hi, quad in turned:
                high = high + (at == jnp.where(quad == float(j), hi, -1.0)).astype(F32)
            block = dot(low.astype(BF), tperm[:, 512 * j : 512 * (j + 1)])
            block = block + dot(high.astype(BF), tperm[:, PW:D])
            opk[b * 128 : (b + 1) * 128, 512 * j : 512 * (j + 1)] = block.astype(BF)

    def tile(ref, i):
        return ref.at[pl.ds(i * PK, PK)]

    def dispatch(first, last):
        for i in range(first, last):
            if i == SELF:
                continue
            k, dy = i // 4, i % 4
            go(send(
                tile(opk, i), tile(rcv, i), ds.at[i], dr.at[i],
                dev(x, y + dy, z + disp(k), c),
            ))

    def from_x(ch, part):
        for k in (1, 3, 2):
            i = part * 9 + ch * 3 + k - 1
            r = owner(zh if part == 0 else 1 - zh, x - k, c)
            arrived(slot(r, ch), xs.at[i], xr.at[i], dev(x + k, y, z, c))
            n = 6 + i
            go(send(slot(r, ch), slot(r, ch), cs.at[n], cr.at[n], core))

    for ch in range(CH):
        from_x(ch, 0)
        arrived(slot(far, ch), zs.at[ch], zr.at[ch], dev(x, y, z + 8, c))
        for k in (1, 3, 2):
            i = 9 + ch * 3 + k - 1
            go(send(slot(far, ch), slot(far, ch), xs.at[i], xr.at[i], dev(x + k, y, z, c)))
        go(send(slot(far, ch), slot(far, ch), cs.at[3 + ch], cr.at[3 + ch], core))
        if ch == 1:
            dispatch(0, SLOTS)
            rcv[SELF * PK : (SELF + 1) * PK, :] = opk[SELF * PK : (SELF + 1) * PK, :]
    for ch in range(CH):
        from_x(ch, 1)
    for ch in range(CH):
        arrived(slot(owner(zh, x, 1 - c), ch), cs.at[ch], cr.at[ch], core)
        arrived(slot(owner(1 - zh, x, 1 - c), ch), cs.at[3 + ch], cr.at[3 + ch], core)
        for part in range(2):
            for k in (1, 2, 3):
                n = 6 + part * 9 + ch * 3 + k - 1
                r = owner(zh if part == 0 else 1 - zh, x - k, 1 - c)
                arrived(slot(r, ch), cs.at[n], cr.at[n], core)
    for cp in keep:
        cp.wait()

    for first, last in GROUPS:
        n = (last - first) * PK
        lo = first * PK
        for i in range(first, last):
            if i == SELF:
                continue
            k, dy = i // 4, i % 4
            arrived(tile(rcv, i), ds.at[i], dr.at[i], dev(x, y + dy, z + disp(k), c))
        a = lax.broadcasted_iota(jnp.int32, (n, n), 0)
        b = lax.broadcasted_iota(jnp.int32, (n, n), 1)
        same = (a // PK) == (b // PK)
        ai, bi = a % PK, b % PK
        xbuf[0:n, 0:PW] = rcv[lo : lo + n, :]
        tail = jnp.zeros((n, 512), F32)
        for j in range(3):
            take = same & (ai // 4 == j) & (bi == 12 + ai % 4)
            tail = tail + dot(
                take.astype(F32).astype(BF), rcv[lo : lo + n, 512 * j : 512 * (j + 1)]
            )
        xbuf[0:n, PW:D] = tail.astype(BF)

        def up(t, carry):
            col = pl.multiple_of(t * 256, 256)
            g = dot(xbuf[0:n, :], gu_all[:, pl.ds(col, 256)])
            u = dot(xbuf[0:n, :], gu_all[:, pl.ds(pl.multiple_of(H + col, 256), 256)])
            hid[0:n, pl.ds(col, 256)] = (g / (1.0 + jnp.exp(-g)) * u).astype(BF)
            return carry

        lax.fori_loop(0, 3, up, 0)

        def down(q):
            w = jnp.concatenate([dn_all[2 * q], dn_all[2 * q + 1]], axis=1)
            return dot(hid[0:n, :], w).astype(BF)

        for q in (6, 7):
            p3[0:n, (q - 6) * 256 : (q - 5) * 256] = down(q)
        for j in range(3):
            put = same & (bi // 4 == j) & (ai == 12 + bi % 4)
            phi[0:n, 512 * j : 512 * (j + 1)] = dot(
                put.astype(F32).astype(BF), p3[0:n, :]
            ).astype(BF)
        real = lax.broadcasted_iota(jnp.int32, (n, 256), 0) % PK < 12

        def pack(q, carry):
            col = pl.multiple_of(q * 256, 256)
            v = jnp.where(real, down(q).astype(F32), phi[0:n, pl.ds(col, 256)].astype(F32))
            ppk[lo : lo + n, pl.ds(col, 256)] = v.astype(BF)
            return carry

        lax.fori_loop(0, 6, pack, 0)
        for i in range(first, last):
            if i == SELF:
                continue
            k, dy = i // 4, i % 4
            go(send(
                tile(ppk, i), tile(ret, i), rs.at[i], rr.at[i],
                dev(x, y - dy, z - disp(k), c),
            ))
    ret[SELF * PK : (SELF + 1) * PK, :] = ppk[SELF * PK : (SELF + 1) * PK, :]

    def put(first, cols, m):
        v = m[0:TOK] + m[TOK : 2 * TOK]
        if first == 0:
            comb[:, cols] = v
        else:
            out[:, cols] = (comb[:, cols] + v).astype(BF)

    for first, last in MIX:
        for i in range(first, last):
            if i == SELF:
                continue
            k, dy = i // 4, i % 4
            arrived(tile(ret, i), rs.at[i], rr.at[i], dev(x, y - dy, z - disp(k), c))
        lo, hi = first * PK, last * PK
        part = jnp.zeros((2 * TOK, 512), F32)
        for j in range(3):
            block = ret[lo:hi, 512 * j : 512 * (j + 1)]
            m = dot(wmix[3, :, lo:hi], block)
            part = part + dot(wmix[j, :, lo:hi], block)
            put(first, slice(512 * j, 512 * (j + 1)), m)
        put(first, slice(PW, D), part)

    for cp in started:
        cp.wait_send()


def restore(held, mixed, out, sems):
    copies = []
    for r in range(NR):
        col = pl.multiple_of(held[r] * DB, DB)
        copies.append(pltpu.make_async_copy(
            mixed.at[:, pl.ds(r * DB, DB)], out.at[:, pl.ds(col, DB)], sems.at[r]
        ))
        copies[-1].start()
    for cp in copies:
        cp.wait()


def local(tokens, routes, route_weight, gate_up_store, down_store, held_bucket):
    vmem = pl.BlockSpec(memory_space=pltpu.VMEM)
    dma = pltpu.SemaphoreType.DMA
    most = max(b - a for a, b in GROUPS) * PK
    mixed = pl.pallas_call(
        kernel,
        out_shape=jax.ShapeDtypeStruct((TOK, D), BF),
        in_specs=[pl.BlockSpec(memory_space=pltpu.SMEM)]
        + [pl.BlockSpec(memory_space=pltpu.HBM)] * 5,
        out_specs=vmem,
        scratch_shapes=[
            pltpu.VMEM((D, 2 * H), BF),
            pltpu.VMEM((NR, H, DB), BF),
            pltpu.VMEM((TOK, D), BF),
            pltpu.VMEM((ROWS, PW), BF),
            pltpu.VMEM((ROWS, PW), BF),
            pltpu.VMEM((ROWS, PW), BF),
            pltpu.VMEM((ROWS, PW), BF),
            pltpu.VMEM((4, 2 * TOK, ROWS), BF),
            pltpu.VMEM((most, D), BF),
            pltpu.VMEM((most, H), BF),
            pltpu.VMEM((most, 512), BF),
            pltpu.VMEM((most, PW), BF),
            pltpu.VMEM((TOK, D), F32),
            pltpu.VMEM((TOK, D), BF),
            pltpu.VMEM((2, TOK), jnp.int32),
            pltpu.VMEM((2, TOK), F32),
            dma((3,)),
            dma((CH,)),
            dma((CH,)), dma((CH,)),
            dma((18,)), dma((18,)),
            dma((24,)), dma((24,)),
            dma((SLOTS,)), dma((SLOTS,)),
            dma((SLOTS,)), dma((SLOTS,)),
        ],
        compiler_params=pltpu.CompilerParams(
            collective_id=0, has_side_effects=True, vmem_limit_bytes=60 << 20
        ),
        name="layer",
    )(
        held_bucket, tokens, routes.T, route_weight.T,
        gate_up_store.reshape(DB, 2 * H), down_store.reshape(H, DB),
    )
    return pl.pallas_call(
        restore,
        out_shape=jax.ShapeDtypeStruct((TOK, D), BF),
        in_specs=[pl.BlockSpec(memory_space=pltpu.SMEM), vmem],
        out_specs=pl.BlockSpec(memory_space=pltpu.HBM),
        scratch_shapes=[dma((NR,))],
        name="restore",
    )(held_bucket, mixed)


def solution(mesh):
    in_specs = (
        P(("rep", "exp"), None),
        P(("rep", "exp"), None),
        P(("rep", "exp"), None),
        P("exp", "rep", None),
        P("exp", None, "rep"),
        P(),
    )
    out_specs = P(("rep", "exp"), None)
    return jax.shard_map(local, mesh=mesh, in_specs=in_specs, out_specs=out_specs, check_vma=False)
```
